32 devices in a mesh: region: 2 (over y), gz: 4 (over z), shot: 2 (over x), gx: 2 (over core).
Axes of the slice: x: 2, y: 2, z: 4, core: 2. Of those that a mesh axis runs over, the one named last changes fastest.
Arguments:
- probes: float32 [64, 16, 16, 128], P(('region', 'gz'), 'gx'), parts along dimension 0, may hold values from -6 to 6
- speed: float32 [64, 16, 16], P(('region', 'gz'), 'gx'), parts along dimension 0, may hold values from 0.02 to 0.18
- incident: float32 [4, 32, 16, 16], P(('region', 'shot'), 'gz', 'gx'), parts along dimension 0, may hold values from -6 to 6
- wavelet: float32 [4, 6], P(('region', 'shot')), parts along dimension 0, may hold values from -1.2 to 1.2
- receivers: int32 [4, 64], P(('region', 'shot')), parts along dimension 0, may hold values from 0 to 8191
Outputs:
- born_field: float32 [4, 32, 16, 16, 128], P(('region', 'shot'), 'gz', 'gx'), parts along dimension 0
- factor: float32 [256, 128], P('region'), parts along dimension 0
The draws below stay inside these ranges and needn't reach their ends.
There are 2 independent parts, one for each index of `region`. The reference program is written for one: setup_inputs(seed, part) draws one part's arguments, and reference() takes and returns one part's arrays. A program takes and returns all parts, laid end to end along the dimension named above; each array names one. Nothing has to cross between parts.
All inputs are finite; a program needn't handle non-finite values.
Results may differ from the reference program's by a relative error of at most 0.00013.
Values sent between devices are 32-bit elements; how exact they have to be, the bound alone decides.
A program may use at most 64 MiB of HBM per device.

```python
import math
import jax
import jax.numpy as jnp
from jax import lax

PROBES = 128
NY = 16
STEPS = 6
RECEIVERS = 64
NZ = 32
NX = 16
SHOTS = 2
CELLS = 8192


def with_ends(values, rng, low, largest):
    index_at = [jax.random.randint(jax.random.fold_in(rng, axis), (), 0, length) for axis, length in enumerate(values.shape)]
    widest = values.shape.index(max(values.shape))
    neighbour = index_at[:widest] + [(index_at[widest] + 1) % values.shape[widest]] + index_at[widest + 1:]
    return values.at[tuple(index_at)].set(low).at[tuple(neighbour)].set(largest)


def level_of(stream_key, extent, shards, least, high):
    level, own = 1.0, jax.random.fold_in(stream_key, 6)
    for axis_at, parts in shards:
        draws = jnp.exp(jax.random.uniform(jax.random.fold_in(own, axis_at), (parts,), jnp.float32, least / len(shards), high / len(shards)))
        level = level * jnp.repeat(draws, extent[axis_at] // parts).reshape([-1 if axis == axis_at else 1 for axis in range(len(extent))])
    return level


def noise(own_key, shape, scale, most, cuts=(), kind=jnp.bfloat16):
    level = level_of(own_key, shape, cuts, -0.22, 0.18) if cuts else 1.0
    drawn = jax.random.normal(own_key, shape, jnp.float32) * scale * level
    return jnp.minimum(jnp.maximum(drawn, -most), most).astype(kind)


def setup_inputs(seed: int = 0, part: int = 0) -> dict:
    streams_of = jax.random.split(jax.random.key(seed), 6)
    part_splits = jax.random.split(jax.random.fold_in(streams_of[5], part), 6)
    return {
        "probes": noise(part_splits[0], (NZ, NX, NY, PROBES), 1.0, 6.0, ((0, 4), (1, 2)), jnp.float32),
        "speed": jnp.clip(jnp.exp(math.log(0.18) - 2.1972246 * jax.random.uniform(part_splits[1], (NZ, NX, NY), jnp.float32) ** level_of(part_splits[1], (NZ, NX, NY), ((0, 4), (1, 2)), -0.2, 0.2)), 0.02, 0.18),
        "incident": noise(part_splits[2], (SHOTS, NZ, NX, NY), 1.0, 6.0, ((0, 2), (1, 4), (2, 2)), jnp.float32),
        "wavelet": noise(part_splits[3], (SHOTS, STEPS), 0.3, 1.2, ((0, 2),), jnp.float32),
        "receivers": with_ends(jax.random.randint(part_splits[4], (SHOTS, RECEIVERS), 0, CELLS), jax.random.fold_in(part_splits[4], 1), 0, CELLS - 1).astype(jnp.int32),
    }


coefficients = (-205.0 / 72.0, 8.0 / 5.0, -1.0 / 5.0, 8.0 / 315.0, -1.0 / 560.0)
damping = 0.1

def stencil(padded):
    inner_z = padded.shape[0] - 8
    inner_x = padded.shape[1] - 8
    inner_y = padded.shape[2] - 8

    def window(shift_z, shift_x, shift_y):
        return padded[4 + shift_z:4 + shift_z + inner_z, 4 + shift_x:4 + shift_x + inner_x, 4 + shift_y:4 + shift_y + inner_y]
    total = 3.0 * coefficients[0] * window(0, 0, 0)
    for offset in range(1, 5):
        pairs = window(offset, 0, 0) + window(-offset, 0, 0)
        pairs = pairs + window(0, offset, 0) + window(0, -offset, 0)
        pairs = pairs + window(0, 0, offset) + window(0, 0, -offset)
        total = total + coefficients[offset] * pairs
    return total

def reference(probes, speed, incident, wavelet, receivers):
    flat_probes = probes.reshape(NZ * NX * NY, PROBES)
    speed_cells = speed[..., None]

    def one_group(inputs):
        source, amplitudes, places = inputs
        drive = source[..., None] * probes
        current = jnp.zeros_like(probes)
        previous = jnp.zeros_like(probes)
        gram = jnp.zeros((PROBES, PROBES), probes.dtype)
        for step in range(STEPS):
            padded = jnp.pad(current, ((4, 4), (4, 4), (4, 4), (0, 0)))
            following = 2.0 * current - previous + speed_cells * stencil(padded) + amplitudes[step] * drive
            previous, current = (current, following)
            rows = jnp.take(current.reshape(NZ * NX * NY, PROBES), places, axis=0)
            gram = gram + jnp.dot(rows.T, rows, precision=lax.Precision.HIGHEST, preferred_element_type=probes.dtype)
        return (current, gram)
    fields, grams = lax.map(one_group, (incident, wavelet, receivers))
    core = jnp.sum(grams, axis=0) / (SHOTS * STEPS * RECEIVERS)
    core = core + damping * jnp.dot(flat_probes.T, flat_probes, precision=lax.Precision.HIGHEST, preferred_element_type=probes.dtype) / CELLS
    lower = jnp.linalg.cholesky(core)
    return (fields, lower.T)
```

```python
import functools

import jax
import jax.numpy as jnp
from jax import lax
from jax.experimental import pallas as pl
from jax.experimental.pallas import tpu as pltpu
from jax.sharding import PartitionSpec as P

coefficients = (-205.0 / 72.0, 8.0 / 5.0, -1.0 / 5.0, 8.0 / 315.0, -1.0 / 560.0)
damping = 0.1
HIGH = lax.Precision.HIGHEST
F32 = jnp.float32
PAD = 8
DEPTH = 4


def gram_of(rows):
    return lax.dot_general(
        rows, rows, (((0,), (0,)), ((), ())), precision=HIGH, preferred_element_type=F32
    )


def kernel(
    sizes,
    wavelet,
    rows_at,
    probes,
    medium,
    group_of,
    out,
    factor,
    fields,
    flat,
    drive,
    speed,
    send,
    recv,
    media,
    picked,
    out_a,
    in_a,
    all_a,
    out_b,
    in_b,
    all_b,
    core,
    pack_s,
    pack_r,
    med_s,
    med_r,
    x_s,
    x_r,
    a_s,
    a_r,
    ba_s,
    ba_r,
    b_s,
    b_r,
    bb_s,
    bb_r,
    o_s,
    o_r,
):
    nz, ns, cz, cx, cy, width, steps, receivers = sizes
    cells = cz * cx
    part = cells // nz
    group = width // nz
    members = nz * 2
    everyone = members * ns
    owners = min(members, receivers // 8)
    own_rows = receivers // owners
    gram_rows = width // owners
    early = (steps - 1) * own_rows

    z = lax.axis_index("gz")
    s = lax.axis_index("shot")
    x = lax.axis_index("gx")
    m = z * 2 + x
    f = s * members + m
    lanes = lax.broadcasted_iota(jnp.int32, (cy, width), 1) // group

    def remote(src, dst, ss, rs, tz, ts, tx):
        return pltpu.make_async_remote_copy(
            src_ref=src,
            dst_ref=dst,
            send_sem=ss,
            recv_sem=rs,
            device_id={"gz": tz, "shot": ts, "gx": tx},
            device_id_type=pl.DeviceIdType.MESH,
        )

    def split(t):
        ts = t // members
        tm = t % members
        return ts, tm, tm // 2, tm % 2

    barrier = pltpu.get_barrier_semaphore()

    def greet(i, c):
        ts, _, tz, tx = split((f + 1 + i) % everyone)
        pl.semaphore_signal(
            barrier,
            inc=1,
            device_id={"gz": tz, "shot": ts, "gx": tx},
            device_id_type=pl.DeviceIdType.MESH,
        )
        return c

    lax.fori_loop(0, everyone - 1, greet, 0)

    def pack(source, zd):
        def body(c, carry):
            acc = None
            for q in range(nz):
                part_q = source(q * part + c)
                shift = (group * (q - zd)) % width
                if shift:
                    part_q = pltpu.roll(part_q, shift, 1)
                acc = part_q if acc is None else jnp.where(lanes == q, part_q, acc)
            send[zd, c] = acc
            return carry

        lax.fori_loop(0, part, body, 0, unroll=2)

    def unpack(target):
        for q in range(nz):

            def body(c, carry):
                acc = None
                for zs in range(nz):
                    piece = recv[zs, c]
                    shift = (group * (zs - q)) % width
                    if shift:
                        piece = pltpu.roll(piece, shift, 1)
                    acc = piece if acc is None else jnp.where(lanes == zs, piece, acc)
                target(q * part + c, acc)
                return carry

            lax.fori_loop(0, part, body, 0, unroll=2)

    for zd in range(nz):
        pack(lambda i: probes[i], zd)
    pl.semaphore_wait(barrier, everyone - 1)

    def exchange_start(ss, rs, land):
        def body(i, c):
            tz = (z + 1 + i) % nz
            remote(send.at[tz], land.at[z], ss.at[tz], rs.at[z], tz, s, x).start()
            return c

        lax.fori_loop(0, nz - 1, body, 0)

    def exchange_wait(ss, rs, land):
        def body(i, c):
            tz = (z + 1 + i) % nz
            remote(send.at[tz], land.at[tz], ss.at[tz], rs.at[tz], tz, s, x).wait()
            return c

        lax.fori_loop(0, nz - 1, body, 0)

    def media_body(wait):
        def body(i, c):
            tz = (z + 1 + i) % nz
            here = media.at[tz] if wait else media.at[z]
            copy = remote(
                medium, here, med_s.at[tz], med_r.at[tz if wait else z], tz, s, x
            )
            if wait:
                copy.wait()
            else:
                copy.start()
            return c

        lax.fori_loop(0, nz - 1, body, 0)

    media_body(False)
    exchange_start(pack_s, pack_r, recv)
    media[z] = medium[...]
    recv[z] = send[z]

    zeros = jnp.zeros((PAD, width), F32)
    blank = jnp.zeros((cy, width), F32)
    outer = (cx + DEPTH) * x
    for n in range(steps - 1):

        def clear(i, c):
            for j in range(cx):
                fields[n, DEPTH + i, DEPTH + j, 0:PAD] = zeros
                fields[n, DEPTH + i, DEPTH + j, PAD + cy : PAD + cy + PAD] = zeros
            for j in range(DEPTH):
                fields[n, DEPTH + i, outer + j, PAD : PAD + cy] = blank
            return c

        lax.fori_loop(0, cz, clear, 0)

    probe_gram = gram_of(probes[...].reshape(cells * cy, width))
    for o in range(owners):
        out_a[o, early : early + gram_rows] = probe_gram[o * gram_rows : (o + 1) * gram_rows]

    media_body(True)
    columns = cx * cy
    zrow = lax.broadcasted_iota(jnp.int32, (nz * cz, width), 0)
    zlane = lax.broadcasted_iota(jnp.int32, (nz * cz, width), 1) // group
    spread_speed = media[:, 0].reshape(nz * cz, columns)
    spread_incident = media[:, 1].reshape(nz * cz, columns)
    for i in range(cz):
        onehot = (zrow == zlane * cz + i).astype(F32)
        for spread, target in ((spread_speed, speed), (spread_incident, drive)):
            target[i * cx : (i + 1) * cx] = lax.dot_general(
                spread, onehot, (((0,), (0,)), ((), ())), precision=HIGH, preferred_element_type=F32
            ).reshape(cx, cy, width)

    exchange_wait(pack_s, pack_r, recv)

    def set_drive(i, value):
        drive[i] = drive[i] * value

    unpack(set_drive)

    low = lanes == 0
    high = lanes == nz - 1

    def put(n, i, j, value):
        flat[pl.ds((i * cx + j) * cy, cy)] = value
        if n < steps - 1:
            fields[n, DEPTH + i, DEPTH + j, PAD : PAD + cy] = value

    def fold(n):
        for i in range(DEPTH):

            def body(j, c):
                rows = pl.ds(PAD, cy)
                below = fields[n, DEPTH + cz - DEPTH + i, DEPTH + j, rows]
                above = fields[n, DEPTH + i, DEPTH + j, rows]
                below = jnp.where(low, 0.0, pltpu.roll(below, group, 1))
                above = jnp.where(high, 0.0, pltpu.roll(above, width - group, 1))
                fields[n, i, DEPTH + j, rows] = below
                fields[n, DEPTH + cz + i, DEPTH + j, rows] = above
                return c

            lax.fori_loop(0, cx, body, 0, unroll=2)

    near = (cx - DEPTH) * (1 - x)
    far = (cx - DEPTH) - near

    def border(n, wait):
        src = fields.at[n, pl.ds(DEPTH, cz), pl.ds(DEPTH + near, DEPTH), pl.ds(PAD, cy)]
        at = (cx + DEPTH) * (1 - x) if wait else (cx + DEPTH) * x
        dst = fields.at[n, pl.ds(DEPTH, cz), pl.ds(at, DEPTH), pl.ds(PAD, cy)]
        return remote(src, dst, x_s.at[n], x_r.at[n], z, s, 1 - x)

    def advance(n, start):
        amplitude = wavelet[0, n]

        def body(i, c):
            for jj in range(DEPTH):
                j = start + jj
                a, b = DEPTH + i, DEPTH + j
                now = fields[n - 1, a, b, PAD : PAD + cy]
                total = (3.0 * coefficients[0]) * now
                for k in range(1, DEPTH + 1):
                    pairs = fields[n - 1, a + k, b, PAD : PAD + cy] + fields[n - 1, a - k, b, PAD : PAD + cy]
                    pairs += fields[n - 1, a, b + k, PAD : PAD + cy] + fields[n - 1, a, b - k, PAD : PAD + cy]
                    pairs += fields[n - 1, a, b, PAD + k : PAD + k + cy] + fields[n - 1, a, b, PAD - k : PAD - k + cy]
                    total += coefficients[k] * pairs
                cell = i * cx + j
                value = 2.0 * now + speed[cell] * total + amplitude * drive[cell]
                if n > 1:
                    value -= fields[n - 2, a, b, PAD : PAD + cy]
                put(n, i, j, value)
            return c

        lax.fori_loop(0, cz, body, 0)

    wide = lax.broadcasted_iota(jnp.int32, (receivers, width), 1) // group

    def pick(n):
        for r in range(receivers):
            picked[r : r + 1] = flat[pl.ds(rows_at[0, r], 1)]
        rows = jnp.where(wide == group_of[...], picked[...], 0.0)
        shift = group
        while shift < width:
            rows = rows + pltpu.roll(rows, shift, 1)
            shift *= 2
        rows = jnp.where(wide == z, rows, 0.0)
        for o in range(owners):
            piece = rows[o * own_rows : (o + 1) * own_rows]
            if n < steps - 1:
                out_a[o, n * own_rows : (n + 1) * own_rows] = piece
            else:
                out_b[o] = piece

    def only(condition, body):
        if owners == members:
            body()
        else:
            pl.when(condition)(body)

    def to_owners(outgoing, incoming, ss, rs, act):
        def body(i, c):
            t = (m + 1 + i) % members

            def start():
                remote(
                    outgoing.at[t], incoming.at[m], ss.at[t], rs.at[m], t // 2, s, t % 2
                ).start()

            def sent():
                remote(
                    outgoing.at[t], incoming.at[m], ss.at[t], rs.at[m], t // 2, s, t % 2
                ).wait_send()

            def arrived():
                remote(
                    outgoing.at[0], incoming.at[t], ss.at[t], rs.at[t], t // 2, s, t % 2
                ).wait_recv()

            if act == "arrived":
                only(m < owners, arrived)
            else:
                only(t < owners, start if act == "start" else sent)
            return c

        lax.fori_loop(0, members - 1, body, 0)

    def sum_up(outgoing, incoming, spread):
        def body():
            incoming[m] = outgoing[m]
            total = incoming[0]
            for t in range(1, members):
                total = total + incoming[t]
            spread[s, m] = total

        only(m < owners, body)

    def to_all(spread, ss, rs, act):
        def body(i, c):
            t = (f + 1 + i) % everyone
            ts, tm, tz, tx = split(t)

            def start():
                remote(spread.at[s, m], spread.at[s, m], ss.at[t], rs.at[f], tz, ts, tx).start()

            def sent():
                remote(spread.at[s, m], spread.at[s, m], ss.at[t], rs.at[f], tz, ts, tx).wait_send()

            def arrived():
                remote(spread.at[ts, tm], spread.at[ts, tm], ss.at[t], rs.at[t], tz, ts, tx).wait_recv()

            if act == "arrived":
                only(tm < owners, arrived)
            else:
                only(m < owners, start if act == "start" else sent)
            return c

        lax.fori_loop(0, everyone - 1, body, 0)

    first = wavelet[0, 0]

    def begin(i, c):
        for j in range(cx):
            put(0, i, j, first * drive[i * cx + j])
        return c

    lax.fori_loop(0, cz, begin, 0)
    border(0, False).start()
    fold(0)
    pick(0)
    for n in range(1, steps):
        advance(n, far)
        if n == steps - 1:
            to_owners(out_a, in_a, a_s, a_r, "arrived")
            sum_up(out_a, in_a, all_a)
            to_all(all_a, ba_s, ba_r, "start")
        border(n - 1, True).wait_recv()
        advance(n, near)
        if n < steps - 1:
            border(n, False).start()
            fold(n)
        pick(n)
        if n == steps - 2:
            to_owners(out_a, in_a, a_s, a_r, "start")
    to_owners(out_b, in_b, b_s, b_r, "start")
    for zd in range(nz):
        pack(lambda i: flat[pl.ds(pl.multiple_of(i * cy, cy), cy)], zd)
    to_owners(out_b, in_b, b_s, b_r, "arrived")
    sum_up(out_b, in_b, all_b)
    to_all(all_b, bb_s, bb_r, "start")

    to_all(all_a, ba_s, ba_r, "arrived")
    sampled = all_a[:, :, 0:early].reshape(ns * owners * early, width)
    probe_part = jnp.zeros((width, width), F32)
    probe_part = all_a[s, :, early : early + gram_rows].reshape(width, width)
    total_cells = float(nz * cz * 2 * cx * cy)
    count = float(ns * steps * receivers)
    core[...] = gram_of(sampled) / count + damping * probe_part / total_cells
    to_all(all_b, bb_s, bb_r, "arrived")
    exchange_start(o_s, o_r, recv)
    recv[z] = send[z]
    core[...] += gram_of(all_b[...].reshape(ns * owners * own_rows, width)) / count

    panel = 8
    row_in = lax.broadcasted_iota(jnp.int32, (panel, width), 0)
    col_in = lax.broadcasted_iota(jnp.int32, (panel, width), 1)
    for p in range(width // panel):
        top = p * panel
        block = core[top : top + panel]
        diag = [
            jnp.broadcast_to(block[:, top + k : top + k + 1], (panel, width)) for k in range(panel)
        ]
        for k in range(panel):
            scale = lax.rsqrt(jnp.broadcast_to(diag[k][k : k + 1], (panel, width)))
            pivot = jnp.broadcast_to(block[k : k + 1], (panel, width)) * scale
            below = jnp.where(row_in > k, diag[k] * scale, 0.0)
            block = jnp.where(row_in == k, pivot, block - below * pivot)
            for l in range(k + 1, panel):
                side = jnp.broadcast_to(diag[l][k : k + 1], (panel, width)) * scale
                diag[l] = diag[l] - below * side
        block = jnp.where(col_in >= row_in + top, block, 0.0)
        factor[top : top + panel] = block
        if top + panel < width:
            rest = lax.dot_general(
                block,
                block,
                (((0,), (0,)), ((), ())),
                precision=HIGH,
                preferred_element_type=F32,
            )
            core[top + panel :] -= rest[top + panel :]

    exchange_wait(o_s, o_r, recv)

    def set_out(i, value):
        out[i] = value

    unpack(set_out)

    for n in range(steps - 1):
        border(n, False).wait_send()
    to_owners(out_a, in_a, a_s, a_r, "sent")
    to_owners(out_b, in_b, b_s, b_r, "sent")
    to_all(all_a, ba_s, ba_r, "sent")
    to_all(all_b, bb_s, bb_r, "sent")


def local(probes, speed, incident, wavelet, receivers):
    cz, cx, cy, width = probes.shape
    nz = lax.axis_size("gz")
    nx = lax.axis_size("gx")
    ns = lax.axis_size("shot")
    steps = wavelet.shape[1]
    count = receivers.shape[1]
    places = receivers[0]
    whole_x = cx * nx
    at_z = places // (whole_x * cy)
    at_x = places // cy % whole_x
    at_y = places % cy
    rows_at = ((at_z % cz * cx + at_x % cx) * cy + at_y)[None]
    inside = at_x // cx == lax.axis_index("gx")
    group_of = jnp.where(inside, at_z // cz, -1)[:, None]
    medium = jnp.stack([speed.reshape(cz, cx * cy), incident[0].reshape(cz, cx * cy)])
    cells = cz * cx
    members = nz * nx
    everyone = members * ns
    owners = min(members, count // 8)
    own_rows = count // owners
    message = (steps - 1) * own_rows + width // owners
    part = cells // nz
    dma = pltpu.SemaphoreType.DMA
    vmem = pl.BlockSpec(memory_space=pltpu.VMEM)
    smem = pl.BlockSpec(memory_space=pltpu.SMEM)
    sizes = (nz, ns, cz, cx, cy, width, steps, count)
    field, factor = pl.pallas_call(
        functools.partial(kernel, sizes),
        out_shape=(
            jax.ShapeDtypeStruct((cells, cy, width), F32),
            jax.ShapeDtypeStruct((width, width), F32),
        ),
        in_specs=[smem, smem, vmem, vmem, vmem],
        out_specs=(vmem, vmem),
        scratch_shapes=[
            pltpu.VMEM((steps - 1, cz + 2 * DEPTH, cx + 2 * DEPTH, cy + 2 * PAD, width), F32),
            pltpu.VMEM((cells * cy, width), F32),
            pltpu.VMEM((cells, cy, width), F32),
            pltpu.VMEM((cells, cy, width), F32),
            pltpu.VMEM((nz, part, cy, width), F32),
            pltpu.VMEM((nz, part, cy, width), F32),
            pltpu.VMEM((nz, 2, cz, cx * cy), F32),
            pltpu.VMEM((count, width), F32),
            pltpu.VMEM((owners, message, width), F32),
            pltpu.VMEM((members, message, width), F32),
            pltpu.VMEM((ns, owners, message, width), F32),
            pltpu.VMEM((owners, own_rows, width), F32),
            pltpu.VMEM((members, own_rows, width), F32),
            pltpu.VMEM((ns, owners, own_rows, width), F32),
            pltpu.VMEM((width, width), F32),
            dma((nz,)),
            dma((nz,)),
            dma((nz,)),
            dma((nz,)),
            dma((steps - 1,)),
            dma((steps - 1,)),
            dma((members,)),
            dma((members,)),
            dma((everyone,)),
            dma((everyone,)),
            dma((members,)),
            dma((members,)),
            dma((everyone,)),
            dma((everyone,)),
            dma((nz,)),
            dma((nz,)),
        ],
        compiler_params=pltpu.CompilerParams(
            collective_id=0, has_side_effects=True, vmem_limit_bytes=48 * 1024 * 1024
        ),
    )(wavelet, rows_at, probes.reshape(cells, cy, width), medium, group_of)
    return (field.reshape(1, cz, cx, cy, width), factor)


def solution(mesh):
    placed = (
        P(("region", "gz"), "gx", None, None),
        P(("region", "gz"), "gx", None),
        P(("region", "shot"), "gz", "gx", None),
        P(("region", "shot"), None),
        P(("region", "shot"), None),
    )
    return jax.shard_map(
        local,
        mesh=mesh,
        in_specs=placed,
        out_specs=(P(("region", "shot"), "gz", "gx", None, None), P("region", None)),
        check_vma=False,
    )
```

```python
import functools

import jax
import jax.numpy as jnp
from jax import lax
from jax.experimental import pallas as pl
from jax.experimental.pallas import tpu as pltpu
from jax.sharding import PartitionSpec as P

coefficients = (-205.0 / 72.0, 8.0 / 5.0, -1.0 / 5.0, 8.0 / 315.0, -1.0 / 560.0)
damping = 0.1
HIGH = lax.Precision.HIGHEST
F32 = jnp.float32
PAD = 8
DEPTH = 4


def gram_of(rows):
    return lax.dot_general(
        rows, rows, (((0,), (0,)), ((), ())), precision=HIGH, preferred_element_type=F32
    )


def kernel(
    sizes,
    wavelet,
    rows_at,
    probes_at,
    medium,
    group_of,
    out,
    factor,
    probes,
    fields,
    flat,
    drive,
    speed,
    send,
    recv,
    media,
    picked,
    out_a,
    in_a,
    partial,
    in_b,
    whole,
    core,
    pack_s,
    pack_r,
    med_s,
    med_r,
    x_s,
    x_r,
    a_s,
    a_r,
    b_s,
    b_r,
    c_s,
    c_r,
    o_s,
    o_r,
    probes_s,
):
    nz, ns, cz, cx, cy, width, steps, receivers = sizes
    cells = cz * cx
    part = cells // nz
    group = width // nz
    members = nz * 2
    everyone = members * ns
    owners = min(members, receivers // 8)
    own_rows = receivers // owners
    rounds = -(-steps // nz)
    keepers = min(everyone, width // 8)
    kept = width // keepers

    z = lax.axis_index("gz")
    s = lax.axis_index("shot")
    x = lax.axis_index("gx")
    m = z * 2 + x
    f = s * members + m
    lanes = lax.broadcasted_iota(jnp.int32, (cy, width), 1) // group

    def remote(src, dst, ss, rs, tz, ts, tx):
        return pltpu.make_async_remote_copy(
            src_ref=src,
            dst_ref=dst,
            send_sem=ss,
            recv_sem=rs,
            device_id={"gz": tz, "shot": ts, "gx": tx},
            device_id_type=pl.DeviceIdType.MESH,
        )

    def split(t):
        ts = t // members
        tm = t % members
        return ts, tm, tm // 2, tm % 2

    probes_copy = pltpu.make_async_copy(probes_at, probes, probes_s)
    probes_copy.start()
    barrier = pltpu.get_barrier_semaphore()

    def greet(i, c):
        ts, _, tz, tx = split((f + 1 + i) % everyone)
        pl.semaphore_signal(
            barrier,
            inc=1,
            device_id={"gz": tz, "shot": ts, "gx": tx},
            device_id_type=pl.DeviceIdType.MESH,
        )
        return c

    lax.fori_loop(0, everyone - 1, greet, 0)

    def turn(blocks):
        blocks = list(blocks)
        half = nz // 2
        while half:
            upper = lax.broadcasted_iota(jnp.int32, blocks[0].shape, 1) // (group * half) % 2 == 1
            for q in range(nz):
                if q & half:
                    continue
                a, b = blocks[q], blocks[q + half]
                if 2 * half == nz:
                    mixed = pltpu.roll(jnp.where(upper, a, b), group * half, 1)
                    blocks[q] = jnp.where(upper, mixed, a)
                    blocks[q + half] = jnp.where(upper, b, mixed)
                else:
                    blocks[q] = jnp.where(upper, pltpu.roll(b, group * half, 1), a)
                    blocks[q + half] = jnp.where(upper, b, pltpu.roll(a, width - group * half, 1))
            half //= 2
        return blocks

    def pack(source):
        def body(c, carry):
            for zd, block in enumerate(turn([source(q * part + c) for q in range(nz)])):
                send[zd, c] = block
            return carry

        lax.fori_loop(0, part, body, 0, unroll=4)

    def unpack(target):
        def body(c, carry):
            for q, block in enumerate(turn([recv[zs, c] for zs in range(nz)])):
                target(q * part + c, block)
            return carry

        lax.fori_loop(0, part, body, 0, unroll=4)

    probes_copy.wait()
    pack(lambda i: probes[i])
    pl.semaphore_wait(barrier, everyone - 1)

    def exchange_start(ss, rs, land):
        def body(i, c):
            tz = (z + 1 + i) % nz
            remote(send.at[tz], land.at[z], ss.at[tz], rs.at[z], tz, s, x).start()
            return c

        lax.fori_loop(0, nz - 1, body, 0)

    def exchange_wait(ss, rs, land):
        def body(i, c):
            tz = (z + 1 + i) % nz
            remote(send.at[tz], land.at[tz], ss.at[tz], rs.at[tz], tz, s, x).wait()
            return c

        lax.fori_loop(0, nz - 1, body, 0)

    def media_body(wait):
        def body(i, c):
            tz = (z + 1 + i) % nz
            here = media.at[tz] if wait else media.at[z]
            copy = remote(
                medium, here, med_s.at[tz], med_r.at[tz if wait else z], tz, s, x
            )
            if wait:
                copy.wait()
            else:
                copy.start()
            return c

        lax.fori_loop(0, nz - 1, body, 0)

    media_body(False)
    exchange_start(pack_s, pack_r, recv)
    media[z] = medium[...]
    recv[z] = send[z]

    zeros = jnp.zeros((PAD, width), F32)
    blank = jnp.zeros((cy, width), F32)
    outer = (cx + DEPTH) * x
    for n in range(steps - 1):

        def clear(i, c):
            for j in range(cx):
                fields[n, DEPTH + i, DEPTH + j, 0:PAD] = zeros
                fields[n, DEPTH + i, DEPTH + j, PAD + cy : PAD + cy + PAD] = zeros
            for j in range(DEPTH):
                fields[n, DEPTH + i, outer + j, PAD : PAD + cy] = blank
            return c

        lax.fori_loop(0, cz, clear, 0)

    total_cells = float(nz * cz * 2 * cx * cy)
    count = float(ns * steps * receivers)
    core[...] = (damping / (ns * total_cells)) * gram_of(probes[...].reshape(cells * cy, width))
    out_a[...] = jnp.zeros_like(out_a)

    media_body(True)
    columns = cx * cy
    zrow = lax.broadcasted_iota(jnp.int32, (nz * cz, width), 0)
    zlane = lax.broadcasted_iota(jnp.int32, (nz * cz, width), 1) // group
    spread_speed = media[:, 0].reshape(nz * cz, columns)
    spread_incident = media[:, 1].reshape(nz * cz, columns)
    for i in range(cz):
        onehot = (zrow == zlane * cz + i).astype(F32)
        for spread, target in ((spread_speed, speed), (spread_incident, drive)):
            target[i * cx : (i + 1) * cx] = lax.dot_general(
                spread, onehot, (((0,), (0,)), ((), ())), precision=HIGH, preferred_element_type=F32
            ).reshape(cx, cy, width)

    exchange_wait(pack_s, pack_r, recv)

    def set_drive(i, value):
        drive[i] = drive[i] * value

    unpack(set_drive)

    low = lanes == 0
    high = lanes == nz - 1
    spans = ((0, DEPTH), (DEPTH, cz - DEPTH), (cz - DEPTH, cz))

    def put(n, span, i, j, value):
        flat[pl.ds((i * cx + j) * cy, cy)] = value
        if n < steps - 1:
            rows = pl.ds(PAD, cy)
            fields[n, DEPTH + i, DEPTH + j, rows] = value
            if span == 0:
                above = jnp.where(high, 0.0, pltpu.roll(value, width - group, 1))
                fields[n, DEPTH + cz + i, DEPTH + j, rows] = above
            if span == 2:
                below = jnp.where(low, 0.0, pltpu.roll(value, group, 1))
                fields[n, DEPTH + i - cz, DEPTH + j, rows] = below

    near = (cx - DEPTH) * (1 - x)
    far = (cx - DEPTH) - near

    def border(n, wait):
        src = fields.at[n, pl.ds(DEPTH, cz), pl.ds(DEPTH + near, DEPTH), pl.ds(PAD, cy)]
        at = (cx + DEPTH) * (1 - x) if wait else (cx + DEPTH) * x
        dst = fields.at[n, pl.ds(DEPTH, cz), pl.ds(at, DEPTH), pl.ds(PAD, cy)]
        return remote(src, dst, x_s.at[n], x_r.at[n], z, s, 1 - x)

    def advance(n, start):
        amplitude = wavelet[0, n]

        def body(span, i, c):
            for jj in range(DEPTH):
                j = start + jj
                a, b = DEPTH + i, DEPTH + j
                now = fields[n - 1, a, b, PAD : PAD + cy]
                total = (3.0 * coefficients[0]) * now
                for k in range(1, DEPTH + 1):
                    pairs = fields[n - 1, a + k, b, PAD : PAD + cy] + fields[n - 1, a - k, b, PAD : PAD + cy]
                    pairs += fields[n - 1, a, b + k, PAD : PAD + cy] + fields[n - 1, a, b - k, PAD : PAD + cy]
                    pairs += fields[n - 1, a, b, PAD + k : PAD + k + cy] + fields[n - 1, a, b, PAD - k : PAD - k + cy]
                    total += coefficients[k] * pairs
                cell = i * cx + j
                value = 2.0 * now + speed[cell] * total + amplitude * drive[cell]
                if n > 1:
                    value -= fields[n - 2, a, b, PAD : PAD + cy]
                put(n, span, i, j, value)
            return c

        for span, (least, most) in enumerate(spans):
            lax.fori_loop(least, most, functools.partial(body, span), 0)

    wide = lax.broadcasted_iota(jnp.int32, (receivers, width), 1) // group

    def pick(n):
        for r in range(receivers):
            picked[r : r + 1] = flat[pl.ds(rows_at[0, r], 1)]
        rows = jnp.where(wide == group_of[...], picked[...], 0.0)
        shift = group
        while shift < width:
            rows = rows + pltpu.roll(rows, shift, 1)
            shift *= 2
        rows = jnp.where(wide == n % nz, rows, 0.0)
        for o in range(owners):
            out_a[o, n // nz] += rows[o * own_rows : (o + 1) * own_rows]

    def only(condition, all_do, body):
        if all_do:
            body()
        else:
            pl.when(condition)(body)

    def slabs(act):
        every = owners == members

        def body(i, c):
            t = (m + 1 + i) % members
            there = (t // 2, s, t % 2)

            def start():
                remote(out_a.at[t], in_a.at[m], a_s.at[t], a_r.at[m], *there).start()

            def sent():
                remote(out_a.at[t], in_a.at[m], a_s.at[t], a_r.at[m], *there).wait_send()

            def arrived():
                remote(out_a.at[0], in_a.at[t], a_s.at[t], a_r.at[t], *there).wait_recv()

            if act == "arrived":
                only(m < owners, every, arrived)
            else:
                only(t < owners, every, start if act == "start" else sent)
            return c

        lax.fori_loop(0, members - 1, body, 0)

    def scatter(act):
        every = keepers == everyone

        def body(i, c):
            t = (f + 1 + i) % everyone
            ts, _, tz, tx = split(t)

            def start():
                remote(partial.at[t], in_b.at[f], b_s.at[t], b_r.at[f], tz, ts, tx).start()

            def sent():
                remote(partial.at[t], in_b.at[f], b_s.at[t], b_r.at[f], tz, ts, tx).wait_send()

            def arrived():
                remote(partial.at[0], in_b.at[t], b_s.at[t], b_r.at[t], tz, ts, tx).wait_recv()

            if act == "arrived":
                only(f < keepers, every, arrived)
            else:
                only(t < keepers, every, start if act == "start" else sent)
            return c

        lax.fori_loop(0, everyone - 1, body, 0)

    def gather(act):
        every = keepers == everyone

        def body(i, c):
            t = (f + 1 + i) % everyone
            ts, _, tz, tx = split(t)

            def start():
                remote(whole.at[f], whole.at[f], c_s.at[t], c_r.at[f], tz, ts, tx).start()

            def sent():
                remote(whole.at[f], whole.at[f], c_s.at[t], c_r.at[f], tz, ts, tx).wait_send()

            def arrived():
                remote(whole.at[t], whole.at[t], c_s.at[t], c_r.at[t], tz, ts, tx).wait_recv()

            if act == "arrived":
                only(t < keepers, every, arrived)
            else:
                only(f < keepers, every, start if act == "start" else sent)
            return c

        lax.fori_loop(0, everyone - 1, body, 0)

    first = wavelet[0, 0]

    def begin(span, i, c):
        for j in range(cx):
            put(0, span, i, j, first * drive[i * cx + j])
        return c

    for span, (least, most) in enumerate(spans):
        lax.fori_loop(least, most, functools.partial(begin, span), 0)
    border(0, False).start()
    pick(0)
    for n in range(1, steps):
        advance(n, far)
        border(n - 1, True).wait_recv()
        advance(n, near)
        if n < steps - 1:
            border(n, False).start()
        pick(n)
    slabs("start")
    pack(lambda i: flat[pl.ds(pl.multiple_of(i * cy, cy), cy)])
    slabs("arrived")

    def own_part():
        in_a[m] = out_a[m]
        total = core[...]
        for h in range(rounds):
            held = turn([in_a[2 * q, h] + in_a[2 * q + 1, h] for q in range(nz)])
            total += gram_of(jnp.concatenate(held, axis=0)) / count
        core[...] = total

    only(m < owners, owners == members, own_part)
    for k in range(keepers):
        partial[k] = core[k * kept : (k + 1) * kept]
    scatter("start")
    scatter("arrived")

    def keep():
        in_b[f] = partial[f]
        total = in_b[0]
        for t in range(1, everyone):
            total = total + in_b[t]
        whole[f] = total

    only(f < keepers, keepers == everyone, keep)
    gather("start")
    gather("arrived")
    exchange_start(o_s, o_r, recv)
    recv[z] = send[z]
    core[...] = whole[...].reshape(width, width)

    panel = 8
    row_in = lax.broadcasted_iota(jnp.int32, (panel, width), 0)
    col_in = lax.broadcasted_iota(jnp.int32, (panel, width), 1)
    for p in range(width // panel):
        top = p * panel
        block = core[top : top + panel]
        diag = [
            jnp.broadcast_to(block[:, top + k : top + k + 1], (panel, width)) for k in range(panel)
        ]
        for k in range(panel):
            scale = lax.rsqrt(jnp.broadcast_to(diag[k][k : k + 1], (panel, width)))
            pivot = jnp.broadcast_to(block[k : k + 1], (panel, width)) * scale
            below = jnp.where(row_in > k, diag[k] * scale, 0.0)
            block = jnp.where(row_in == k, pivot, block - below * pivot)
            for l in range(k + 1, panel):
                side = jnp.broadcast_to(diag[l][k : k + 1], (panel, width)) * scale
                diag[l] = diag[l] - below * side
        block = jnp.where(col_in >= row_in + top, block, 0.0)
        factor[top : top + panel] = block
        if top + panel < width:
            rest = lax.dot_general(
                block,
                block,
                (((0,), (0,)), ((), ())),
                precision=HIGH,
                preferred_element_type=F32,
            )
            core[top + panel :] -= rest[top + panel :]

    exchange_wait(o_s, o_r, recv)

    def set_out(i, value):
        out[i] = value

    unpack(set_out)

    for n in range(steps - 1):
        border(n, False).wait_send()
    slabs("sent")
    scatter("sent")
    gather("sent")


def local(probes, speed, incident, wavelet, receivers):
    cz, cx, cy, width = probes.shape
    nz = lax.axis_size("gz")
    nx = lax.axis_size("gx")
    ns = lax.axis_size("shot")
    steps = wavelet.shape[1]
    count = receivers.shape[1]
    places = receivers[0]
    whole_x = cx * nx
    at_z = places // (whole_x * cy)
    at_x = places // cy % whole_x
    at_y = places % cy
    rows_at = ((at_z % cz * cx + at_x % cx) * cy + at_y)[None]
    inside = at_x // cx == lax.axis_index("gx")
    group_of = jnp.where(inside, at_z // cz, -1)[:, None]
    medium = jnp.stack([speed.reshape(cz, cx * cy), incident[0].reshape(cz, cx * cy)])
    cells = cz * cx
    members = nz * nx
    everyone = members * ns
    owners = min(members, count // 8)
    own_rows = count // owners
    rounds = -(-steps // nz)
    keepers = min(everyone, width // 8)
    part = cells // nz
    dma = pltpu.SemaphoreType.DMA
    vmem = pl.BlockSpec(memory_space=pltpu.VMEM)
    smem = pl.BlockSpec(memory_space=pltpu.SMEM)
    sizes = (nz, ns, cz, cx, cy, width, steps, count)
    field, factor = pl.pallas_call(
        functools.partial(kernel, sizes),
        out_shape=(
            jax.ShapeDtypeStruct((cells, cy, width), F32),
            jax.ShapeDtypeStruct((width, width), F32),
        ),
        in_specs=[smem, smem, pl.BlockSpec(memory_space=pl.ANY), vmem, vmem],
        out_specs=(vmem, vmem),
        scratch_shapes=[
            pltpu.VMEM((cells, cy, width), F32),
            pltpu.VMEM((steps - 1, cz + 2 * DEPTH, cx + 2 * DEPTH, cy + 2 * PAD, width), F32),
            pltpu.VMEM((cells * cy, width), F32),
            pltpu.VMEM((cells, cy, width), F32),
            pltpu.VMEM((cells, cy, width), F32),
            pltpu.VMEM((nz, part, cy, width), F32),
            pltpu.VMEM((nz, part, cy, width), F32),
            pltpu.VMEM((nz, 2, cz, cx * cy), F32),
            pltpu.VMEM((count, width), F32),
            pltpu.VMEM((owners, rounds, own_rows, width), F32),
            pltpu.VMEM((members, rounds, own_rows, width), F32),
            pltpu.VMEM((keepers, width // keepers, width), F32),
            pltpu.VMEM((everyone, width // keepers, width), F32),
            pltpu.VMEM((keepers, width // keepers, width), F32),
            pltpu.VMEM((width, width), F32),
            dma((nz,)),
            dma((nz,)),
            dma((nz,)),
            dma((nz,)),
            dma((steps - 1,)),
            dma((steps - 1,)),
            dma((members,)),
            dma((members,)),
            dma((everyone,)),
            dma((everyone,)),
            dma((everyone,)),
            dma((everyone,)),
            dma((nz,)),
            dma((nz,)),
            dma,
        ],
        compiler_params=pltpu.CompilerParams(
            collective_id=0, has_side_effects=True, vmem_limit_bytes=48 * 1024 * 1024
        ),
    )(wavelet, rows_at, probes.reshape(cells, cy, width), medium, group_of)
    return (field.reshape(1, cz, cx, cy, width), factor)


def solution(mesh):
    placed = (
        P(("region", "gz"), "gx", None, None),
        P(("region", "gz"), "gx", None),
        P(("region", "shot"), "gz", "gx", None),
        P(("region", "shot"), None),
        P(("region", "shot"), None),
    )
    return jax.shard_map(
        local,
        mesh=mesh,
        in_specs=placed,
        out_specs=(P(("region", "shot"), "gz", "gx", None, None), P("region", None)),
        check_vma=False,
    )
```

```python
import functools

import jax
import jax.numpy as jnp
from jax import lax
from jax.experimental import pallas as pl
from jax.experimental.pallas import tpu as pltpu
from jax.sharding import PartitionSpec as P

coefficients = (-205.0 / 72.0, 8.0 / 5.0, -1.0 / 5.0, 8.0 / 315.0, -1.0 / 560.0)
damping = 0.1
HIGH = lax.Precision.HIGHEST
F32 = jnp.float32
PAD = 8
DEPTH = 4


def gram_of(rows):
    return lax.dot_general(
        rows, rows, (((0,), (0,)), ((), ())), precision=HIGH, preferred_element_type=F32
    )


def kernel(
    sizes,
    wavelet,
    rows_at,
    probes_at,
    medium,
    group_of,
    out,
    factor,
    probes,
    fields,
    flat,
    drive,
    speed,
    send,
    recv,
    media,
    picked,
    out_a,
    in_a,
    partial,
    in_b,
    whole,
    core,
    pack_s,
    pack_r,
    med_s,
    med_r,
    x_s,
    x_r,
    a_s,
    a_r,
    b_s,
    b_r,
    c_s,
    c_r,
    o_s,
    o_r,
    probes_s,
):
    nz, ns, cz, cx, cy, width, steps, receivers = sizes
    cells = cz * cx
    part = cells // nz
    group = width // nz
    members = nz * 2
    everyone = members * ns
    owners = min(members, receivers // 8)
    own_rows = receivers // owners
    rounds = -(-steps // nz)
    keepers = min(everyone, width // 8)
    kept = width // keepers

    z = lax.axis_index("gz")
    s = lax.axis_index("shot")
    x = lax.axis_index("gx")
    m = z * 2 + x
    f = s * members + m
    lanes = lax.broadcasted_iota(jnp.int32, (cy, width), 1) // group

    def remote(src, dst, ss, rs, tz, ts, tx):
        return pltpu.make_async_remote_copy(
            src_ref=src,
            dst_ref=dst,
            send_sem=ss,
            recv_sem=rs,
            device_id={"gz": tz, "shot": ts, "gx": tx},
            device_id_type=pl.DeviceIdType.MESH,
        )

    def partners(shots, body):
        def at(tz, near):
            for ds in range(ns if shots else 1):
                ts = lax.rem(s + ds, ns) if ds else s
                for dx in range(2):
                    if ds or dx or not near:
                        body(tz, ts, 1 - x if dx else x)

        if nz <= 4:
            for dz in range(1, nz):
                at(lax.rem(z + dz, nz), False)
        else:

            def step(dz, c):
                at(lax.rem(z + dz, nz), False)
                return c

            lax.fori_loop(1, nz, step, 0)
        at(z, True)

    probes_copy = pltpu.make_async_copy(probes_at, probes, probes_s)
    probes_copy.start()
    barrier = pltpu.get_barrier_semaphore()

    def greet(tz, ts, tx):
        pl.semaphore_signal(
            barrier,
            inc=1,
            device_id={"gz": tz, "shot": ts, "gx": tx},
            device_id_type=pl.DeviceIdType.MESH,
        )

    partners(True, greet)

    def turn(blocks):
        blocks = list(blocks)
        half = nz // 2
        while half:
            upper = lax.broadcasted_iota(jnp.int32, blocks[0].shape, 1) // (group * half) % 2 == 1
            for q in range(nz):
                if q & half:
                    continue
                a, b = blocks[q], blocks[q + half]
                if 2 * half == nz:
                    mixed = pltpu.roll(jnp.where(upper, a, b), group * half, 1)
                    blocks[q] = jnp.where(upper, mixed, a)
                    blocks[q + half] = jnp.where(upper, b, mixed)
                else:
                    blocks[q] = jnp.where(upper, pltpu.roll(b, group * half, 1), a)
                    blocks[q + half] = jnp.where(upper, b, pltpu.roll(a, width - group * half, 1))
            half //= 2
        return blocks

    def pack(source):
        def body(c, carry):
            for zd, block in enumerate(turn([source(q * part + c) for q in range(nz)])):
                send[zd, c] = block
            return carry

        lax.fori_loop(0, part, body, 0, unroll=4)

    def unpack(target):
        def body(c, carry):
            for q, block in enumerate(turn([recv[zs, c] for zs in range(nz)])):
                target(q * part + c, block)
            return carry

        lax.fori_loop(0, part, body, 0, unroll=4)

    probes_copy.wait()
    pack(lambda i: probes[i])
    pl.semaphore_wait(barrier, everyone - 1)

    def along(body):
        for dz in range(1, nz):
            body(lax.rem(z + dz, nz))

    def exchange_start(ss, rs, land):
        def body(tz):
            remote(send.at[tz], land.at[z], ss.at[tz], rs.at[z], tz, s, x).start()

        along(body)

    def exchange_wait(ss, rs, land):
        def body(tz):
            remote(send.at[tz], land.at[tz], ss.at[tz], rs.at[tz], tz, s, x).wait()

        along(body)

    def media_body(wait):
        def body(tz):
            here = media.at[tz] if wait else media.at[z]
            copy = remote(
                medium, here, med_s.at[tz], med_r.at[tz if wait else z], tz, s, x
            )
            if wait:
                copy.wait()
            else:
                copy.start()

        along(body)

    media_body(False)
    exchange_start(pack_s, pack_r, recv)
    media[z] = medium[...]
    recv[z] = send[z]

    zeros = jnp.zeros((PAD, width), F32)
    blank = jnp.zeros((cy, width), F32)
    outer = (cx + DEPTH) * x
    for n in range(steps - 1):

        def clear(i, c):
            for j in range(cx):
                fields[n, DEPTH + i, DEPTH + j, 0:PAD] = zeros
                fields[n, DEPTH + i, DEPTH + j, PAD + cy : PAD + cy + PAD] = zeros
            for j in range(DEPTH):
                fields[n, DEPTH + i, outer + j, PAD : PAD + cy] = blank
            return c

        lax.fori_loop(0, cz, clear, 0)

    total_cells = float(nz * cz * 2 * cx * cy)
    count = float(ns * steps * receivers)
    core[...] = (damping / (ns * total_cells)) * gram_of(probes[...].reshape(cells * cy, width))
    out_a[...] = jnp.zeros_like(out_a)

    media_body(True)
    columns = cx * cy
    zrow = lax.broadcasted_iota(jnp.int32, (nz * cz, width), 0)
    zlane = lax.broadcasted_iota(jnp.int32, (nz * cz, width), 1) // group
    spread_speed = media[:, 0].reshape(nz * cz, columns)
    spread_incident = media[:, 1].reshape(nz * cz, columns)
    for i in range(cz):
        onehot = (zrow == zlane * cz + i).astype(F32)
        for spread, target in ((spread_speed, speed), (spread_incident, drive)):
            target[i * cx : (i + 1) * cx] = lax.dot_general(
                spread, onehot, (((0,), (0,)), ((), ())), precision=HIGH, preferred_element_type=F32
            ).reshape(cx, cy, width)

    exchange_wait(pack_s, pack_r, recv)

    def set_drive(i, value):
        drive[i] = drive[i] * value

    unpack(set_drive)

    low = lanes == 0
    high = lanes == nz - 1
    spans = ((0, DEPTH), (DEPTH, cz - DEPTH), (cz - DEPTH, cz))

    def put(n, span, i, j, value):
        flat[pl.ds((i * cx + j) * cy, cy)] = value
        if n < steps - 1:
            rows = pl.ds(PAD, cy)
            fields[n, DEPTH + i, DEPTH + j, rows] = value
            if span == 0:
                above = jnp.where(high, 0.0, pltpu.roll(value, width - group, 1))
                fields[n, DEPTH + cz + i, DEPTH + j, rows] = above
            if span == 2:
                below = jnp.where(low, 0.0, pltpu.roll(value, group, 1))
                fields[n, DEPTH + i - cz, DEPTH + j, rows] = below

    near = (cx - DEPTH) * (1 - x)
    far = (cx - DEPTH) - near

    def border(n, wait):
        src = fields.at[n, pl.ds(DEPTH, cz), pl.ds(DEPTH + near, DEPTH), pl.ds(PAD, cy)]
        at = (cx + DEPTH) * (1 - x) if wait else (cx + DEPTH) * x
        dst = fields.at[n, pl.ds(DEPTH, cz), pl.ds(at, DEPTH), pl.ds(PAD, cy)]
        return remote(src, dst, x_s.at[n], x_r.at[n], z, s, 1 - x)

    def advance(n, start):
        amplitude = wavelet[0, n]

        def body(span, i, c):
            for jj in range(DEPTH):
                j = start + jj
                a, b = DEPTH + i, DEPTH + j
                now = fields[n - 1, a, b, PAD : PAD + cy]
                total = (3.0 * coefficients[0]) * now
                for k in range(1, DEPTH + 1):
                    pairs = fields[n - 1, a + k, b, PAD : PAD + cy] + fields[n - 1, a - k, b, PAD : PAD + cy]
                    pairs += fields[n - 1, a, b + k, PAD : PAD + cy] + fields[n - 1, a, b - k, PAD : PAD + cy]
                    pairs += fields[n - 1, a, b, PAD + k : PAD + k + cy] + fields[n - 1, a, b, PAD - k : PAD - k + cy]
                    total += coefficients[k] * pairs
                cell = i * cx + j
                value = 2.0 * now + speed[cell] * total + amplitude * drive[cell]
                if n > 1:
                    value -= fields[n - 2, a, b, PAD : PAD + cy]
                put(n, span, i, j, value)
            return c

        for span, (least, most) in enumerate(spans):
            lax.fori_loop(least, most, functools.partial(body, span), 0)

    wide = lax.broadcasted_iota(jnp.int32, (receivers, width), 1) // group

    def pick(n):
        for r in range(receivers):
            picked[r : r + 1] = flat[pl.ds(rows_at[0, r], 1)]
        rows = jnp.where(wide == group_of[...], picked[...], 0.0)
        shift = group
        while shift < width:
            rows = rows + pltpu.roll(rows, shift, 1)
            shift *= 2
        rows = jnp.where(wide == n % nz, rows, 0.0)
        for o in range(owners):
            out_a[o, n // nz] += rows[o * own_rows : (o + 1) * own_rows]

    def only(condition, all_do, body):
        if all_do:
            body()
        else:
            pl.when(condition)(body)

    def slabs(act):
        every = owners == members

        def body(*there):
            t = there[0] * 2 + there[2]

            def start():
                remote(out_a.at[t], in_a.at[m], a_s.at[t], a_r.at[m], *there).start()

            def sent():
                remote(out_a.at[t], in_a.at[m], a_s.at[t], a_r.at[m], *there).wait_send()

            def arrived():
                remote(out_a.at[0], in_a.at[t], a_s.at[t], a_r.at[t], *there).wait_recv()

            if act == "arrived":
                only(m < owners, every, arrived)
            else:
                only(t < owners, every, start if act == "start" else sent)

        partners(False, body)

    def scatter(act):
        every = keepers == everyone

        def body(tz, ts, tx):
            t = ts * members + tz * 2 + tx

            def start():
                remote(partial.at[t], in_b.at[f], b_s.at[t], b_r.at[f], tz, ts, tx).start()

            def sent():
                remote(partial.at[t], in_b.at[f], b_s.at[t], b_r.at[f], tz, ts, tx).wait_send()

            def arrived():
                remote(partial.at[0], in_b.at[t], b_s.at[t], b_r.at[t], tz, ts, tx).wait_recv()

            if act == "arrived":
                only(f < keepers, every, arrived)
            else:
                only(t < keepers, every, start if act == "start" else sent)

        partners(True, body)

    def gather(act):
        every = keepers == everyone

        def body(tz, ts, tx):
            t = ts * members + tz * 2 + tx

            def start():
                remote(whole.at[f], whole.at[f], c_s.at[t], c_r.at[f], tz, ts, tx).start()

            def sent():
                remote(whole.at[f], whole.at[f], c_s.at[t], c_r.at[f], tz, ts, tx).wait_send()

            def arrived():
                remote(whole.at[t], whole.at[t], c_s.at[t], c_r.at[t], tz, ts, tx).wait_recv()

            if act == "arrived":
                only(t < keepers, every, arrived)
            else:
                only(f < keepers, every, start if act == "start" else sent)

        partners(True, body)

    first = wavelet[0, 0]

    def begin(span, i, c):
        for j in range(cx):
            put(0, span, i, j, first * drive[i * cx + j])
        return c

    for span, (least, most) in enumerate(spans):
        lax.fori_loop(least, most, functools.partial(begin, span), 0)
    border(0, False).start()
    pick(0)
    for n in range(1, steps):
        advance(n, far)
        border(n - 1, True).wait_recv()
        advance(n, near)
        if n < steps - 1:
            border(n, False).start()
        pick(n)
    slabs("start")
    pack(lambda i: flat[pl.ds(pl.multiple_of(i * cy, cy), cy)])
    slabs("arrived")

    def own_part():
        in_a[m] = out_a[m]
        total = core[...]
        for h in range(rounds):
            held = turn([in_a[2 * q, h] + in_a[2 * q + 1, h] for q in range(nz)])
            total += gram_of(jnp.concatenate(held, axis=0)) / count
        core[...] = total

    only(m < owners, owners == members, own_part)
    for k in range(keepers):
        partial[k] = core[k * kept : (k + 1) * kept]
    scatter("start")
    scatter("arrived")

    def keep():
        in_b[f] = partial[f]
        total = in_b[0]
        for t in range(1, everyone):
            total = total + in_b[t]
        whole[f] = total

    only(f < keepers, keepers == everyone, keep)
    gather("start")
    exchange_start(o_s, o_r, recv)
    recv[z] = send[z]
    gather("arrived")
    core[...] = whole[...].reshape(width, width)

    panel = 8
    row_in = lax.broadcasted_iota(jnp.int32, (panel, width), 0)
    col_in = lax.broadcasted_iota(jnp.int32, (panel, width), 1)
    for p in range(width // panel):
        top = p * panel
        block = core[top : top + panel]
        diag = [
            jnp.broadcast_to(block[:, top + k : top + k + 1], (panel, width)) for k in range(panel)
        ]
        for k in range(panel):
            scale = lax.rsqrt(jnp.broadcast_to(diag[k][k : k + 1], (panel, width)))
            pivot = jnp.broadcast_to(block[k : k + 1], (panel, width)) * scale
            below = jnp.where(row_in > k, diag[k] * scale, 0.0)
            block = jnp.where(row_in == k, pivot, block - below * pivot)
            for l in range(k + 1, panel):
                side = jnp.broadcast_to(diag[l][k : k + 1], (panel, width)) * scale
                diag[l] = diag[l] - below * side
        block = jnp.where(col_in >= row_in + top, block, 0.0)
        factor[top : top + panel] = block
        if top + panel < width:
            rest = lax.dot_general(
                block,
                block,
                (((0,), (0,)), ((), ())),
                precision=HIGH,
                preferred_element_type=F32,
            )
            core[top + panel :] -= rest[top + panel :]

    exchange_wait(o_s, o_r, recv)

    def set_out(i, value):
        out[i] = value

    unpack(set_out)

    for n in range(steps - 1):
        border(n, False).wait_send()
    slabs("sent")
    scatter("sent")
    gather("sent")


def local(probes, speed, incident, wavelet, receivers):
    cz, cx, cy, width = probes.shape
    nz = lax.axis_size("gz")
    nx = lax.axis_size("gx")
    ns = lax.axis_size("shot")
    steps = wavelet.shape[1]
    count = receivers.shape[1]
    places = receivers[0]
    whole_x = cx * nx
    at_z = places // (whole_x * cy)
    at_x = places // cy % whole_x
    at_y = places % cy
    rows_at = ((at_z % cz * cx + at_x % cx) * cy + at_y)[None]
    inside = at_x // cx == lax.axis_index("gx")
    group_of = jnp.where(inside, at_z // cz, -1)[:, None]
    medium = jnp.stack([speed.reshape(cz, cx * cy), incident[0].reshape(cz, cx * cy)])
    cells = cz * cx
    members = nz * nx
    everyone = members * ns
    owners = min(members, count // 8)
    own_rows = count // owners
    rounds = -(-steps // nz)
    keepers = min(everyone, width // 8)
    part = cells // nz
    dma = pltpu.SemaphoreType.DMA
    vmem = pl.BlockSpec(memory_space=pltpu.VMEM)
    smem = pl.BlockSpec(memory_space=pltpu.SMEM)
    sizes = (nz, ns, cz, cx, cy, width, steps, count)
    field, factor = pl.pallas_call(
        functools.partial(kernel, sizes),
        out_shape=(
            jax.ShapeDtypeStruct((cells, cy, width), F32),
            jax.ShapeDtypeStruct((width, width), F32),
        ),
        in_specs=[smem, smem, pl.BlockSpec(memory_space=pl.ANY), vmem, vmem],
        out_specs=(vmem, vmem),
        scratch_shapes=[
            pltpu.VMEM((cells, cy, width), F32),
            pltpu.VMEM((steps - 1, cz + 2 * DEPTH, cx + 2 * DEPTH, cy + 2 * PAD, width), F32),
            pltpu.VMEM((cells * cy, width), F32),
            pltpu.VMEM((cells, cy, width), F32),
            pltpu.VMEM((cells, cy, width), F32),
            pltpu.VMEM((nz, part, cy, width), F32),
            pltpu.VMEM((nz, part, cy, width), F32),
            pltpu.VMEM((nz, 2, cz, cx * cy), F32),
            pltpu.VMEM((count, width), F32),
            pltpu.VMEM((owners, rounds, own_rows, width), F32),
            pltpu.VMEM((members, rounds, own_rows, width), F32),
            pltpu.VMEM((keepers, width // keepers, width), F32),
            pltpu.VMEM((everyone, width // keepers, width), F32),
            pltpu.VMEM((keepers, width // keepers, width), F32),
            pltpu.VMEM((width, width), F32),
            dma((nz,)),
            dma((nz,)),
            dma((nz,)),
            dma((nz,)),
            dma((steps - 1,)),
            dma((steps - 1,)),
            dma((members,)),
            dma((members,)),
            dma((everyone,)),
            dma((everyone,)),
            dma((everyone,)),
            dma((everyone,)),
            dma((nz,)),
            dma((nz,)),
            dma,
        ],
        compiler_params=pltpu.CompilerParams(
            collective_id=0, has_side_effects=True, vmem_limit_bytes=48 * 1024 * 1024
        ),
    )(wavelet, rows_at, probes.reshape(cells, cy, width), medium, group_of)
    return (field.reshape(1, cz, cx, cy, width), factor)


def solution(mesh):
    placed = (
        P(("region", "gz"), "gx", None, None),
        P(("region", "gz"), "gx", None),
        P(("region", "shot"), "gz", "gx", None),
        P(("region", "shot"), None),
        P(("region", "shot"), None),
    )
    return jax.shard_map(
        local,
        mesh=mesh,
        in_specs=placed,
        out_specs=(P(("region", "shot"), "gz", "gx", None, None), P("region", None)),
        check_vma=False,
    )
```
